32 devices in a mesh: groups: 2 (over y), wide: 4 (over z), loop: 4 (over x, core).
Axes of the slice: x: 2, y: 2, z: 4, core: 2. Of those that a mesh axis runs over, the one named last changes fastest.
Arguments:
- image_embed: bfloat16 [2048, 1152], P(('groups', 'wide', 'loop')), parts along dimension 0, may hold values from -24 to 24
- text_embed: bfloat16 [2048, 1152], P(('groups', 'wide', 'loop')), parts along dimension 0, may hold values from -24 to 24
- pair_index: int32 [2048], P(('groups', 'wide', 'loop')), parts along dimension 0, may hold values from 0 to 1023, as said below
- logit_scale: float32 [1], replicated, may hold values from 5 to 15
- logit_bias: float32 [1], replicated, may hold values from -3 to -1
Outputs:
- text_grad: float32 [2048, 1152], P(('groups', 'wide', 'loop')), parts along dimension 0
- mean_loss: float32 [2], P('groups'), parts along dimension 0
The draws below stay inside these ranges and needn't reach their ends.
There are 2 independent parts, one for each index of `groups`. The reference program is written for one: setup_inputs(seed, part) draws one part's arguments, and reference() takes and returns one part's arrays. A program takes and returns all parts, laid end to end along the dimension named above; an argument that names none is the same for every part. Nothing has to cross between parts.
Inputs may be any that keep to these rules, and one draw needn't show every extreme that they name: A permutation of 0 to 1023: image i is paired with text pair_index[i].
All inputs are finite; a program needn't handle non-finite values.
Results may differ from the reference program's by a relative error of at most 0.00049.
Values may be sent and summed in bfloat16 or wider, within the bound.
A program may use at most 64 MiB of HBM per device.

```python
import math
import jax
import jax.numpy as jnp
from jax import lax

D = 1152
ROWS_DEV = 64
PAIRS = 1024
N_LOOP = 4


def shared_order(key):
    return jax.random.permutation(jax.random.fold_in(key, 101), PAIRS).astype(jnp.int32)


def shared_latent(key, centre_weight, spread_weight):
    cluster_total = max(PAIRS // 32, 4)
    labels = jax.random.randint(jax.random.fold_in(key, 102), (PAIRS,), 0, cluster_total)
    centres = jax.random.normal(jax.random.fold_in(key, 103), (cluster_total, D), jnp.float32)
    spread = jax.random.normal(jax.random.fold_in(key, 104), (PAIRS, D), jnp.float32)
    return centre_weight * jnp.take(centres, labels, axis=0) + spread_weight * spread


def common_direction(key):
    return jax.random.normal(jax.random.fold_in(key, 105), (1, D), jnp.float32)


def block_weight(low, loop_step, wide_step):
    row_place = jnp.arange(PAIRS, dtype=jnp.int32)
    blocks = row_place // ROWS_DEV
    loop_place = (blocks % N_LOOP).astype(jnp.float32) / float(max(N_LOOP - 1, 1))
    wide_place = (blocks // N_LOOP % 2).astype(jnp.float32)
    return (low + loop_step * loop_place + wide_step * wide_place)[:, None]


def add_noise(key, latent, noise_scale, scale_low, scale_high, limit):
    noise = noise_scale * jax.random.normal(jax.random.fold_in(key, 201), latent.shape, jnp.float32)
    row_log = jax.random.uniform(jax.random.fold_in(key, 202), (latent.shape[0], 1), jnp.float32, jnp.log(scale_low), jnp.log(scale_high))
    return jnp.clip((latent + noise) * jnp.exp(row_log), -limit, limit)


def draw_pair_index(key, part):
    return shared_order(key)


def draw_text_embed(key, part):
    common = common_direction(key)
    latent = shared_latent(key, 0.55, 0.55) + block_weight(0.1, 0.35, 0.2) * common
    key = jax.random.fold_in(key, 7)
    values = add_noise(key, latent, 0.63, 1.0, 1.0, 8.0)
    return values.astype(jnp.bfloat16)


def draw_image_embed(key, part):
    order = shared_order(key)
    common = common_direction(key)
    paired = jnp.take(shared_latent(key, 0.55, 0.55), order, axis=0) + block_weight(0.1, 0.35, 0.2) * common
    key = jax.random.fold_in(key, 9)
    values = add_noise(key, paired, 0.63, 1.0, 1.0, 8.0)
    return values.astype(jnp.bfloat16)


def setup_inputs(seed: int = 0, part: int = 0) -> dict:
    arg_keys = jax.random.split(jax.random.key(seed), 6)
    own_keys = jax.random.split(jax.random.fold_in(arg_keys[5], part), 6)
    image_embed = draw_image_embed(jax.random.fold_in(jax.random.fold_in(arg_keys[5], part), 71), part)
    text_embed = draw_text_embed(jax.random.fold_in(jax.random.fold_in(arg_keys[5], part), 71), part)
    pair_index = draw_pair_index(jax.random.fold_in(jax.random.fold_in(arg_keys[5], part), 71), part)
    logit_scale = jnp.clip(jax.random.uniform(arg_keys[3], (1,), jnp.float32, 5.0, 15.0), 5.0, 15.0)
    logit_bias = jnp.clip(jax.random.uniform(arg_keys[4], (1,), jnp.float32, -3.0, -1.0), -3.0, -1.0)
    return {"image_embed": image_embed, "text_embed": text_embed, "pair_index": pair_index, "logit_scale": logit_scale, "logit_bias": logit_bias}


epsilon = 1e-06

def normalize(values):
    wide_values = values.astype(jnp.float32)
    inverse = lax.rsqrt(lax.optimization_barrier(jnp.sum(wide_values * wide_values, axis=1, keepdims=True)) + epsilon)
    return (wide_values * inverse, inverse)

def pair_terms(text_block, first_row, image_bf, pairs, scale_value, bias_value):
    scores = lax.dot_general(text_block, image_bf, (((1,), (1,)), ((), ())), preferred_element_type=jnp.float32)
    logits = scale_value * scores + bias_value
    columns = first_row + lax.broadcasted_iota(jnp.int32, (text_block.shape[0], 1), 0)
    positive = pairs[None, :] == columns
    signed = jnp.where(positive, logits, -logits)
    loss_part = -jnp.sum(jax.nn.log_sigmoid(signed))
    weights = (scale_value * (jax.nn.sigmoid(logits) - positive.astype(jnp.float32))).astype(jnp.bfloat16)
    partial_sum = jnp.dot(weights, image_bf, preferred_element_type=jnp.float32)
    return (loss_part, partial_sum)

def reference(image_embed, text_embed, pair_index, logit_scale, logit_bias):
    image_unit, _ = normalize(image_embed)
    image_bf = image_unit.astype(jnp.bfloat16)
    text_hat, inverse = normalize(text_embed)
    text_bf = text_hat.astype(jnp.bfloat16)
    block_rows = math.gcd(PAIRS, 512)
    block_count = PAIRS // block_rows
    starts = jnp.arange(block_count, dtype=jnp.int32) * block_rows

    def block_terms(inputs):
        text_block, first_row = inputs
        return pair_terms(text_block, first_row, image_bf, pair_index, logit_scale[0], logit_bias[0])
    losses, partials = lax.map(block_terms, (text_bf.reshape(block_count, block_rows, D), starts))
    unit_grad = partials.reshape(PAIRS, D)
    along = lax.optimization_barrier(jnp.sum(text_hat * unit_grad, axis=1, keepdims=True))
    text_grad = (unit_grad - text_hat * along) * inverse
    mean_loss = jnp.reshape(jnp.sum(losses) / (float(PAIRS) * float(PAIRS)), (1,)).astype(jnp.float32)
    return (text_grad, mean_loss)
```

```python
import functools

import jax
import jax.numpy as jnp
from jax import lax
from jax.experimental import pallas as pl
from jax.experimental.pallas import tpu as pltpu
from jax.sharding import PartitionSpec as P

epsilon = 1e-06
MESH = pl.DeviceIdType.MESH


def passed_along(block, axis, distance):
    devices = range(lax.axis_size(axis))
    route = [((i - distance) % len(devices), i) for i in devices]
    return lax.ppermute(block, axis, route)


def normalize(values):
    wide_values = values.astype(jnp.float32)
    inverse = lax.rsqrt(jnp.sum(wide_values * wide_values, axis=1, keepdims=True) + epsilon)
    return (wide_values * inverse, inverse)


def pair_terms(text_block, first_row, image_bf, pairs, scale_value, bias_value):
    scores = lax.dot_general(
        text_block, image_bf, (((1,), (1,)), ((), ())), preferred_element_type=jnp.float32
    )
    logits = scale_value * scores + bias_value
    columns = first_row + lax.broadcasted_iota(jnp.int32, (text_block.shape[0], 1), 0)
    positive = pairs[None, :] == columns
    signed = jnp.where(positive, logits, -logits)
    loss_part = -jnp.sum(jax.nn.log_sigmoid(signed))
    weights = (scale_value * (jax.nn.sigmoid(logits) - positive.astype(jnp.float32))).astype(
        jnp.bfloat16
    )
    partial_sum = jnp.dot(weights, image_bf, preferred_element_type=jnp.float32)
    return (loss_part, partial_sum)


def ring_shards(image_embed, text_embed, pair_index, logit_scale, logit_bias):
    local_rows = text_embed.shape[0]
    width_dim = text_embed.shape[1]
    loop_size = lax.axis_size("loop")
    loop_index = lax.axis_index("loop")
    wide_index = lax.axis_index("wide")
    scale_value = logit_scale[0]
    bias_value = logit_bias[0]
    image_unit, _ = normalize(image_embed)
    image_bf = image_unit.astype(jnp.bfloat16)
    text_hat, inverse = normalize(text_embed)
    text_bf = text_hat.astype(jnp.bfloat16)
    group_first = wide_index * loop_size * local_rows
    gathered, gathered_pairs = (
        lax.all_gather(image_bf, "wide", axis=0, tiled=True),
        lax.all_gather(pair_index, "wide", axis=0, tiled=True),
    )
    loss_sum = jnp.zeros((), jnp.float32)
    text_block = text_bf
    accumulated = jnp.zeros((local_rows, width_dim), jnp.float32)
    for cycle_step in range(loop_size):
        owner_block = (loop_index - cycle_step) % loop_size
        first_row = group_first + owner_block * local_rows
        loss_part, partial_sum = pair_terms(
            text_block, first_row, gathered, gathered_pairs, scale_value, bias_value
        )
        loss_sum = loss_sum + loss_part
        accumulated = accumulated + partial_sum
        if cycle_step + 1 < loop_size:
            text_block = passed_along(text_block, "loop", 1)
            accumulated = passed_along(accumulated, "loop", 1)
    unit_grad = passed_along(accumulated, "loop", 1)
    along = jnp.sum(text_hat * unit_grad, axis=1, keepdims=True)
    text_grad = (unit_grad - text_hat * along) * inverse
    pairs_total = float(local_rows * lax.axis_size("wide") * loop_size)
    total_loss = lax.psum(loss_sum, ("wide", "loop"))
    mean_loss = jnp.reshape(total_loss / (pairs_total * pairs_total), (1,))
    return (text_grad, mean_loss)


def gather_kernel(
    rows,
    image_ref,
    text_ref,
    pair_ref,
    scale_ref,
    bias_ref,
    grad_ref,
    loss_ref,
    gathered,
    pair_all,
    pair_rows,
    loss_all,
    loss_mine,
    text_bf,
    total,
    send_sem,
    recv_sem,
    small_send,
    small_recv,
):
    wide, loop = lax.axis_index("wide"), lax.axis_index("loop")
    me = wide * 4 + loop
    sibling = loop + 1 - 2 * (loop % 2)
    across = (loop + 2) % 4
    across_sibling = (sibling + 2) % 4
    interior = (wide % 3) != 0
    ends = (wide % 3) == 0
    high = wide // 2
    source = [wide, wide + 1 - 2 * (wide % 2), 2 - high, 3 - 3 * high]
    middle = 3 - wide
    outer = (wide - 1) * 3

    barrier = pltpu.get_barrier_semaphore()

    def peer(step):
        other = (me + step) % 16
        return {"wide": other // 4, "loop": other % 4}

    for step in range(1, 16):
        pl.semaphore_signal(barrier, inc=1, device_id=peer(step), device_id_type=MESH)

    def block(place, column):
        slot = place * 4 + column
        return slot, gathered.at[pl.ds(pl.multiple_of(slot * rows, rows), rows), :]

    image = image_ref[...].astype(jnp.float32)
    image_inverse = lax.rsqrt(jnp.sum(image * image, axis=1, keepdims=True) + epsilon)
    gathered[pl.ds(pl.multiple_of(me * rows, rows), rows), :] = (image * image_inverse).astype(
        jnp.bfloat16
    )
    own_pairs = jnp.concatenate([pair_ref[...], jnp.zeros((1, 128 - rows), jnp.int32)], axis=1)
    pair_all[me] = own_pairs
    pl.semaphore_wait(barrier, 15)

    def send(number, place, column, to):
        slot, view = block(place, column)
        copy = pltpu.make_async_remote_copy(
            src_ref=view,
            dst_ref=view,
            send_sem=send_sem.at[number],
            recv_sem=recv_sem.at[slot],
            device_id=to,
            device_id_type=MESH,
        )
        copy.start()

    def sent(number):
        view = gathered.at[pl.ds(0, rows), :]
        pltpu.make_async_copy(view, view, send_sem.at[number]).wait()

    def arrived(place, column):
        slot, view = block(place, column)
        pltpu.make_async_copy(view, view, recv_sem.at[slot]).wait()

    send(0, wide, loop, {"wide": source[1], "loop": loop})

    @pl.when(interior)
    def _():
        send(1, wide, loop, {"wide": middle, "loop": loop})

    send(2, wide, loop, {"wide": wide, "loop": across})
    send(3, wide, loop, {"wide": wide, "loop": sibling})
    for step in range(1, 16):
        pltpu.make_async_remote_copy(
            src_ref=pair_all.at[me],
            dst_ref=pair_all.at[me],
            send_sem=small_send.at[0],
            recv_sem=small_recv.at[0],
            device_id=peer(step),
            device_id_type=MESH,
        ).start()

    text = text_ref[...].astype(jnp.float32)
    inverse = lax.rsqrt(jnp.sum(text * text, axis=1, keepdims=True) + epsilon)
    text_bf[...] = (text * inverse).astype(jnp.bfloat16)
    scale_value = scale_ref[0]
    bias_value = bias_ref[0]
    fifteen = pair_all.at[pl.ds(0, 15)]
    pltpu.make_async_copy(fifteen, fifteen, small_recv.at[0]).wait()
    for place in range(4):
        pair_rows[place : place + 1, :] = jnp.concatenate(
            [pair_all[place * 4 + column][:, :rows] for column in range(4)], axis=1
        )

    def pass_on(k):
        arrived(source[k], loop)

        @pl.when(interior)
        def _():
            send(4 + k, source[k], loop, {"wide": middle if k == 1 else outer, "loop": loop})

        send(8 + k, source[k], loop, {"wide": wide, "loop": across})
        send(12 + k, source[k], loop, {"wide": wide, "loop": sibling})

    def pass_across(k):
        arrived(source[k], across)
        send(16 + k, source[k], across, {"wide": wide, "loop": sibling})
        arrived(source[k], sibling)
        arrived(source[k], across_sibling)

    columns = me * rows + lax.broadcasted_iota(jnp.int32, (rows, 4 * rows), 0)

    def terms(k):
        place = source[k]
        images = gathered[pl.ds(pl.multiple_of(place * 4 * rows, 4 * rows), 4 * rows), :]
        scores = lax.dot_general(
            text_bf[...], images, (((1,), (1,)), ((), ())), preferred_element_type=jnp.float32
        )
        logits = scale_value * scores + bias_value
        positive = pair_rows[pl.ds(place, 1), :] == columns
        small = jnp.exp(-jnp.abs(logits))
        above = 1.0 + small
        log_above = jnp.where(above == 1.0, small, jnp.log(above) * small / jnp.where(above == 1.0, 1.0, above - 1.0))
        loss = log_above + jnp.maximum(jnp.where(positive, -logits, logits), 0.0)
        sigmoid = jnp.where(logits >= 0.0, 1.0, small) / above
        weights = (scale_value * (sigmoid - jnp.where(positive, 1.0, 0.0))).astype(jnp.bfloat16)
        tile = loss[:, :128] + loss[:, 128:]
        tile = jnp.sum(tile.reshape(rows // 8, 8, 128), axis=0)
        return tile, weights, images

    def accumulate(k, weights, images):
        partial = jnp.dot(weights, images, preferred_element_type=jnp.float32)
        if k == 0:
            total[...] = partial
        else:
            total[...] += partial

    pass_on(1)

    @pl.when(interior)
    def _():
        pass_on(2)

    pass_across(0)
    tile, weights, images = terms(0)
    accumulate(0, weights, images)
    loss_tile = tile

    @pl.when(ends)
    def _():
        pass_on(2)

    @pl.when(interior)
    def _():
        pass_on(3)

    pass_across(1)
    tile, weights, images = terms(1)
    accumulate(1, weights, images)
    loss_tile += tile

    @pl.when(ends)
    def _():
        pass_on(3)

    pass_across(2)
    tile, weights, images = terms(2)
    accumulate(2, weights, images)
    loss_tile += tile

    pass_across(3)
    tile, weights, images = terms(3)
    loss_tile += tile
    loss_mine[...] = loss_tile
    for step in range(1, 16):
        pltpu.make_async_remote_copy(
            src_ref=loss_mine,
            dst_ref=loss_all.at[step - 1],
            send_sem=small_send.at[1],
            recv_sem=small_recv.at[1],
            device_id=peer(step),
            device_id_type=MESH,
        ).start()
    unit_grad = total[...] + jnp.dot(weights, images, preferred_element_type=jnp.float32)
    text = text_ref[...].astype(jnp.float32)
    inverse = lax.rsqrt(jnp.sum(text * text, axis=1, keepdims=True) + epsilon)
    text_hat = text * inverse
    along = jnp.sum(text_hat * unit_grad, axis=1, keepdims=True)
    grad_ref[...] = (unit_grad - text_hat * along) * inverse

    for number in (0, 2, 3, 9, 10, 11, 13, 14, 15, 16, 17, 18, 19):
        sent(number)

    @pl.when(interior)
    def _():
        for number in (1, 5, 6, 7):
            sent(number)

    pltpu.make_async_copy(fifteen, fifteen, small_send.at[0]).wait()
    pltpu.make_async_copy(loss_all, loss_all, small_send.at[1]).wait()
    pltpu.make_async_copy(loss_all, loss_all, small_recv.at[1]).wait()
    whole = loss_mine[...] + jnp.sum(loss_all[...], axis=0)
    loss_ref[0] = jnp.sum(whole) * (1.0 / float((16 * rows) ** 2))


def gather_shards(image_embed, text_embed, pair_index, logit_scale, logit_bias):
    rows, width = text_embed.shape
    vmem = pl.BlockSpec(memory_space=pltpu.VMEM)
    smem = pl.BlockSpec(memory_space=pltpu.SMEM)
    return pl.pallas_call(
        functools.partial(gather_kernel, rows),
        out_shape=(
            jax.ShapeDtypeStruct((rows, width), jnp.float32),
            jax.ShapeDtypeStruct((1,), jnp.float32),
        ),
        in_specs=[vmem, vmem, vmem, smem, smem],
        out_specs=(vmem, smem),
        scratch_shapes=[
            pltpu.VMEM((16 * rows, width), jnp.bfloat16),
            pltpu.VMEM((16, 1, 128), jnp.int32),
            pltpu.VMEM((8, 4 * rows), jnp.int32),
            pltpu.VMEM((15, 8, 128), jnp.float32),
            pltpu.VMEM((8, 128), jnp.float32),
            pltpu.VMEM((rows, width), jnp.bfloat16),
            pltpu.VMEM((rows, width), jnp.float32),
            pltpu.SemaphoreType.DMA((20,)),
            pltpu.SemaphoreType.DMA((16,)),
            pltpu.SemaphoreType.DMA((2,)),
            pltpu.SemaphoreType.DMA((2,)),
        ],
        compiler_params=pltpu.CompilerParams(
            collective_id=0, has_side_effects=True, vmem_limit_bytes=32 * 1024 * 1024
        ),
    )(image_embed, text_embed, pair_index.reshape(1, rows), logit_scale, logit_bias)


def solution(mesh):
    small = mesh.shape["wide"] == 4 and mesh.shape["loop"] == 4
    return jax.shard_map(
        gather_shards if small else ring_shards,
        mesh=mesh,
        in_specs=(
            P(("groups", "wide", "loop"), None),
            P(("groups", "wide", "loop"), None),
            P(("groups", "wide", "loop")),
            P(),
            P(),
        ),
        out_specs=(P(("groups", "wide", "loop"), None), P("groups")),
        check_vma=False,
    )
```

```python
import functools

import jax
import jax.numpy as jnp
from jax import lax
from jax.experimental import pallas as pl
from jax.experimental.pallas import tpu as pltpu
from jax.sharding import PartitionSpec as P

epsilon = 1e-06
MESH = pl.DeviceIdType.MESH


def passed_along(block, axis, distance):
    devices = range(lax.axis_size(axis))
    route = [((i - distance) % len(devices), i) for i in devices]
    return lax.ppermute(block, axis, route)


def normalize(values):
    wide_values = values.astype(jnp.float32)
    inverse = lax.rsqrt(jnp.sum(wide_values * wide_values, axis=1, keepdims=True) + epsilon)
    return (wide_values * inverse, inverse)


def pair_terms(text_block, first_row, image_bf, pairs, scale_value, bias_value):
    scores = lax.dot_general(
        text_block, image_bf, (((1,), (1,)), ((), ())), preferred_element_type=jnp.float32
    )
    logits = scale_value * scores + bias_value
    columns = first_row + lax.broadcasted_iota(jnp.int32, (text_block.shape[0], 1), 0)
    positive = pairs[None, :] == columns
    signed = jnp.where(positive, logits, -logits)
    loss_part = -jnp.sum(jax.nn.log_sigmoid(signed))
    weights = (scale_value * (jax.nn.sigmoid(logits) - positive.astype(jnp.float32))).astype(
        jnp.bfloat16
    )
    partial_sum = jnp.dot(weights, image_bf, preferred_element_type=jnp.float32)
    return (loss_part, partial_sum)


def ring_shards(image_embed, text_embed, pair_index, logit_scale, logit_bias):
    local_rows = text_embed.shape[0]
    width_dim = text_embed.shape[1]
    loop_size = lax.axis_size("loop")
    loop_index = lax.axis_index("loop")
    wide_index = lax.axis_index("wide")
    scale_value = logit_scale[0]
    bias_value = logit_bias[0]
    image_unit, _ = normalize(image_embed)
    image_bf = image_unit.astype(jnp.bfloat16)
    text_hat, inverse = normalize(text_embed)
    text_bf = text_hat.astype(jnp.bfloat16)
    group_first = wide_index * loop_size * local_rows
    gathered, gathered_pairs = (
        lax.all_gather(image_bf, "wide", axis=0, tiled=True),
        lax.all_gather(pair_index, "wide", axis=0, tiled=True),
    )
    loss_sum = jnp.zeros((), jnp.float32)
    text_block = text_bf
    accumulated = jnp.zeros((local_rows, width_dim), jnp.float32)
    for cycle_step in range(loop_size):
        owner_block = (loop_index - cycle_step) % loop_size
        first_row = group_first + owner_block * local_rows
        loss_part, partial_sum = pair_terms(
            text_block, first_row, gathered, gathered_pairs, scale_value, bias_value
        )
        loss_sum = loss_sum + loss_part
        accumulated = accumulated + partial_sum
        if cycle_step + 1 < loop_size:
            text_block = passed_along(text_block, "loop", 1)
            accumulated = passed_along(accumulated, "loop", 1)
    unit_grad = passed_along(accumulated, "loop", 1)
    along = jnp.sum(text_hat * unit_grad, axis=1, keepdims=True)
    text_grad = (unit_grad - text_hat * along) * inverse
    pairs_total = float(local_rows * lax.axis_size("wide") * loop_size)
    total_loss = lax.psum(loss_sum, ("wide", "loop"))
    mean_loss = jnp.reshape(total_loss / (pairs_total * pairs_total), (1,))
    return (text_grad, mean_loss)


PARTS = 2


def gather_kernel(
    rows,
    image_hbm,
    text_hbm,
    pair_hbm,
    scale_ref,
    bias_ref,
    grad_ref,
    loss_ref,
    gathered,
    image_raw,
    text_raw,
    pair_raw,
    pair_all,
    pair_rows,
    loss_all,
    loss_mine,
    text_bf,
    total,
    load_sem,
    send_sem,
    recv_sem,
    small_send,
    small_recv,
):
    wide, loop = lax.axis_index("wide"), lax.axis_index("loop")
    me = wide * 4 + loop
    sibling = loop + 1 - 2 * (loop % 2)
    across = (loop + 2) % 4
    across_sibling = (sibling + 2) % 4
    interior = (wide % 3) != 0
    ends = (wide % 3) == 0
    high = wide // 2
    source = [wide, wide + 1 - 2 * (wide % 2), 2 - high, 3 - 3 * high]
    middle = 3 - wide
    outer = (wide - 1) * 3
    size = rows // PARTS
    parts = range(PARTS)

    load_image = pltpu.make_async_copy(image_hbm, image_raw, load_sem.at[0])
    load_text = pltpu.make_async_copy(text_hbm, text_raw, load_sem.at[1])
    load_pair = pltpu.make_async_copy(pair_hbm, pair_raw, load_sem.at[2])
    load_image.start()
    load_pair.start()
    load_text.start()

    barrier = pltpu.get_barrier_semaphore()

    def peer(step):
        other = (me + step) % 16
        return {"wide": other // 4, "loop": other % 4}

    for step in range(1, 16):
        pl.semaphore_signal(barrier, inc=1, device_id=peer(step), device_id_type=MESH)

    def block(place, column, part):
        slot = (place * 4 + column) * PARTS + part
        return slot, gathered.at[pl.ds(pl.multiple_of(slot * size, size), size), :]

    load_image.wait()
    image = image_raw[...].astype(jnp.float32)
    image_inverse = lax.rsqrt(jnp.sum(image * image, axis=1, keepdims=True) + epsilon)
    gathered[pl.ds(pl.multiple_of(me * rows, rows), rows), :] = (image * image_inverse).astype(
        jnp.bfloat16
    )
    load_pair.wait()
    pair_all[me] = jnp.concatenate([pair_raw[...], jnp.zeros((1, 128 - rows), jnp.int32)], axis=1)
    pl.semaphore_wait(barrier, 15)

    def send(number, place, column, part, to):
        slot, view = block(place, column, part)
        pltpu.make_async_remote_copy(
            src_ref=view,
            dst_ref=view,
            send_sem=send_sem.at[number * PARTS + part],
            recv_sem=recv_sem.at[slot],
            device_id=to,
            device_id_type=MESH,
        ).start()

    def sent(number):
        view = gathered.at[pl.ds(0, size), :]
        for part in parts:
            pltpu.make_async_copy(view, view, send_sem.at[number * PARTS + part]).wait()

    def arrived(place, column, part):
        slot, view = block(place, column, part)
        pltpu.make_async_copy(view, view, recv_sem.at[slot]).wait()

    for part in parts:
        send(0, wide, loop, part, {"wide": source[1], "loop": loop})

        @pl.when(interior)
        def _():
            send(1, wide, loop, part, {"wide": middle, "loop": loop})

        send(2, wide, loop, part, {"wide": wide, "loop": across})
    for part in parts:
        send(3, wide, loop, part, {"wide": wide, "loop": sibling})
    for step in range(1, 16):
        pltpu.make_async_remote_copy(
            src_ref=pair_all.at[me],
            dst_ref=pair_all.at[me],
            send_sem=small_send.at[0],
            recv_sem=small_recv.at[0],
            device_id=peer(step),
            device_id_type=MESH,
        ).start()

    load_text.wait()
    text = text_raw[...].astype(jnp.float32)
    inverse = lax.rsqrt(jnp.sum(text * text, axis=1, keepdims=True) + epsilon)
    text_bf[...] = (text * inverse).astype(jnp.bfloat16)
    scale_value = scale_ref[0]
    bias_value = bias_ref[0]

    def pass_on(k, part):
        arrived(source[k], loop, part)

        @pl.when(interior)
        def _():
            send(
                4 + k,
                source[k],
                loop,
                part,
                {"wide": middle if k == 1 else outer, "loop": loop},
            )

        send(8 + k, source[k], loop, part, {"wide": wide, "loop": across})
        send(12 + k, source[k], loop, part, {"wide": wide, "loop": sibling})

    def pass_across(k, part):
        arrived(source[k], across, part)
        send(16 + k, source[k], across, part, {"wide": wide, "loop": sibling})

    def siblings(k):
        for part in parts:
            arrived(source[k], sibling, part)
        for part in parts:
            arrived(source[k], across_sibling, part)

    columns = me * rows + lax.broadcasted_iota(jnp.int32, (rows, 4 * rows), 0)

    def terms(k):
        place = source[k]
        images = gathered[pl.ds(pl.multiple_of(place * 4 * rows, 4 * rows), 4 * rows), :]
        scores = lax.dot_general(
            text_bf[...], images, (((1,), (1,)), ((), ())), preferred_element_type=jnp.float32
        )
        logits = scale_value * scores + bias_value
        positive = pair_rows[pl.ds(place, 1), :] == columns
        small = jnp.exp(-jnp.abs(logits))
        above = 1.0 + small
        lost = above == 1.0
        log_above = jnp.where(
            lost, small, jnp.log(above) * small / jnp.where(lost, 1.0, above - 1.0)
        )
        loss = log_above + jnp.maximum(jnp.where(positive, -logits, logits), 0.0)
        sigmoid = jnp.where(logits >= 0.0, 1.0, small) / above
        weights = (scale_value * (sigmoid - jnp.where(positive, 1.0, 0.0))).astype(jnp.bfloat16)
        tile = loss[:, :128] + loss[:, 128:]
        tile = jnp.sum(tile.reshape(rows // 8, 8, 128), axis=0)
        return tile, weights, images

    def accumulate(k, weights, images):
        partial = jnp.dot(weights, images, preferred_element_type=jnp.float32)
        if k == 0:
            total[...] = partial
        else:
            total[...] += partial

    for part in parts:
        pass_on(1, part)

        @pl.when(interior)
        def _():
            pass_on(2, part)

        pass_across(0, part)
    fifteen = pair_all.at[pl.ds(0, 15)]
    pltpu.make_async_copy(fifteen, fifteen, small_recv.at[0]).wait()
    for place in range(4):
        pair_rows[place : place + 1, :] = jnp.concatenate(
            [pair_all[place * 4 + column][:, :rows] for column in range(4)], axis=1
        )
    siblings(0)
    tile, weights, images = terms(0)
    accumulate(0, weights, images)
    loss_tile = tile

    for part in parts:

        @pl.when(ends)
        def _():
            pass_on(2, part)

        @pl.when(interior)
        def _():
            pass_on(3, part)

        pass_across(1, part)
    siblings(1)
    tile, weights, images = terms(1)
    accumulate(1, weights, images)
    loss_tile += tile

    for part in parts:

        @pl.when(ends)
        def _():
            pass_on(3, part)

        pass_across(2, part)
    siblings(2)
    tile, weights, images = terms(2)
    accumulate(2, weights, images)
    loss_tile += tile

    for part in parts:
        pass_across(3, part)
    siblings(3)
    tile, weights, images = terms(3)
    loss_tile += tile
    loss_mine[...] = jnp.sum(loss_tile, axis=0, keepdims=True)
    for step in range(1, 16):
        pltpu.make_async_remote_copy(
            src_ref=loss_mine,
            dst_ref=loss_all.at[step - 1],
            send_sem=small_send.at[1],
            recv_sem=small_recv.at[1],
            device_id=peer(step),
            device_id_type=MESH,
        ).start()
    unit_grad = total[...] + jnp.dot(weights, images, preferred_element_type=jnp.float32)
    text = text_raw[...].astype(jnp.float32)
    inverse = lax.rsqrt(jnp.sum(text * text, axis=1, keepdims=True) + epsilon)
    text_hat = text * inverse
    along = jnp.sum(text_hat * unit_grad, axis=1, keepdims=True)
    grad_ref[...] = (unit_grad - text_hat * along) * inverse

    for number in (0, 2, 3, 9, 10, 11, 13, 14, 15, 16, 17, 18, 19):
        sent(number)

    @pl.when(interior)
    def _():
        for number in (1, 5, 6, 7):
            sent(number)

    pltpu.make_async_copy(fifteen, fifteen, small_send.at[0]).wait()
    pltpu.make_async_copy(loss_all, loss_all, small_send.at[1]).wait()
    pltpu.make_async_copy(loss_all, loss_all, small_recv.at[1]).wait()
    whole = loss_mine[...] + jnp.sum(loss_all[...], axis=0)
    loss_ref[0] = jnp.sum(whole) * (1.0 / float((16 * rows) ** 2))


def gather_shards(image_embed, text_embed, pair_index, logit_scale, logit_bias):
    rows, width = text_embed.shape
    vmem = pl.BlockSpec(memory_space=pltpu.VMEM)
    smem = pl.BlockSpec(memory_space=pltpu.SMEM)
    hbm = pl.BlockSpec(memory_space=pltpu.HBM)
    return pl.pallas_call(
        functools.partial(gather_kernel, rows),
        out_shape=(
            jax.ShapeDtypeStruct((rows, width), jnp.float32),
            jax.ShapeDtypeStruct((1,), jnp.float32),
        ),
        in_specs=[hbm, hbm, hbm, smem, smem],
        out_specs=(vmem, smem),
        scratch_shapes=[
            pltpu.VMEM((16 * rows, width), jnp.bfloat16),
            pltpu.VMEM((rows, width), jnp.bfloat16),
            pltpu.VMEM((rows, width), jnp.bfloat16),
            pltpu.VMEM((1, rows), jnp.int32),
            pltpu.VMEM((16, 1, 128), jnp.int32),
            pltpu.VMEM((8, 4 * rows), jnp.int32),
            pltpu.VMEM((15, 1, 128), jnp.float32),
            pltpu.VMEM((1, 128), jnp.float32),
            pltpu.VMEM((rows, width), jnp.bfloat16),
            pltpu.VMEM((rows, width), jnp.float32),
            pltpu.SemaphoreType.DMA((3,)),
            pltpu.SemaphoreType.DMA((20 * PARTS,)),
            pltpu.SemaphoreType.DMA((16 * PARTS,)),
            pltpu.SemaphoreType.DMA((2,)),
            pltpu.SemaphoreType.DMA((2,)),
        ],
        compiler_params=pltpu.CompilerParams(
            collective_id=0, has_side_effects=True, vmem_limit_bytes=60 * 1024 * 1024
        ),
    )(image_embed, text_embed, pair_index.reshape(1, rows), logit_scale, logit_bias)


def solution(mesh):
    small = mesh.shape["wide"] == 4 and mesh.shape["loop"] == 4
    return jax.shard_map(
        gather_shards if small else ring_shards,
        mesh=mesh,
        in_specs=(
            P(("groups", "wide", "loop"), None),
            P(("groups", "wide", "loop"), None),
            P(("groups", "wide", "loop")),
            P(),
            P(),
        ),
        out_specs=(P(("groups", "wide", "loop"), None), P("groups")),
        check_vma=False,
    )
```

```python
import functools

import jax
import jax.numpy as jnp
from jax import lax
from jax.experimental import pallas as pl
from jax.experimental.pallas import tpu as pltpu
from jax.sharding import PartitionSpec as P

epsilon = 1e-06
MESH = pl.DeviceIdType.MESH


def passed_along(block, axis, distance):
    devices = range(lax.axis_size(axis))
    route = [((i - distance) % len(devices), i) for i in devices]
    return lax.ppermute(block, axis, route)


def normalize(values):
    wide_values = values.astype(jnp.float32)
    inverse = lax.rsqrt(jnp.sum(wide_values * wide_values, axis=1, keepdims=True) + epsilon)
    return (wide_values * inverse, inverse)


def pair_terms(text_block, first_row, image_bf, pairs, scale_value, bias_value):
    scores = lax.dot_general(
        text_block, image_bf, (((1,), (1,)), ((), ())), preferred_element_type=jnp.float32
    )
    logits = scale_value * scores + bias_value
    columns = first_row + lax.broadcasted_iota(jnp.int32, (text_block.shape[0], 1), 0)
    positive = pairs[None, :] == columns
    signed = jnp.where(positive, logits, -logits)
    loss_part = -jnp.sum(jax.nn.log_sigmoid(signed))
    weights = (scale_value * (jax.nn.sigmoid(logits) - positive.astype(jnp.float32))).astype(
        jnp.bfloat16
    )
    partial_sum = jnp.dot(weights, image_bf, preferred_element_type=jnp.float32)
    return (loss_part, partial_sum)


def ring_shards(image_embed, text_embed, pair_index, logit_scale, logit_bias):
    local_rows = text_embed.shape[0]
    width_dim = text_embed.shape[1]
    loop_size = lax.axis_size("loop")
    loop_index = lax.axis_index("loop")
    wide_index = lax.axis_index("wide")
    scale_value = logit_scale[0]
    bias_value = logit_bias[0]
    image_unit, _ = normalize(image_embed)
    image_bf = image_unit.astype(jnp.bfloat16)
    text_hat, inverse = normalize(text_embed)
    text_bf = text_hat.astype(jnp.bfloat16)
    group_first = wide_index * loop_size * local_rows
    gathered, gathered_pairs = (
        lax.all_gather(image_bf, "wide", axis=0, tiled=True),
        lax.all_gather(pair_index, "wide", axis=0, tiled=True),
    )
    loss_sum = jnp.zeros((), jnp.float32)
    text_block = text_bf
    accumulated = jnp.zeros((local_rows, width_dim), jnp.float32)
    for cycle_step in range(loop_size):
        owner_block = (loop_index - cycle_step) % loop_size
        first_row = group_first + owner_block * local_rows
        loss_part, partial_sum = pair_terms(
            text_block, first_row, gathered, gathered_pairs, scale_value, bias_value
        )
        loss_sum = loss_sum + loss_part
        accumulated = accumulated + partial_sum
        if cycle_step + 1 < loop_size:
            text_block = passed_along(text_block, "loop", 1)
            accumulated = passed_along(accumulated, "loop", 1)
    unit_grad = passed_along(accumulated, "loop", 1)
    along = jnp.sum(text_hat * unit_grad, axis=1, keepdims=True)
    text_grad = (unit_grad - text_hat * along) * inverse
    pairs_total = float(local_rows * lax.axis_size("wide") * loop_size)
    total_loss = lax.psum(loss_sum, ("wide", "loop"))
    mean_loss = jnp.reshape(total_loss / (pairs_total * pairs_total), (1,))
    return (text_grad, mean_loss)


PARTS = 2


def gather_kernel(
    rows,
    image_hbm,
    text_hbm,
    pair_hbm,
    scale_hbm,
    bias_hbm,
    grad_ref,
    loss_ref,
    gathered,
    image_raw,
    text_raw,
    pair_raw,
    pair_all,
    pair_rows,
    loss_all,
    loss_mine,
    text_bf,
    total,
    scale_ref,
    bias_ref,
    load_sem,
    send_sem,
    recv_sem,
    small_send,
    small_recv,
):
    wide, loop = lax.axis_index("wide"), lax.axis_index("loop")
    me = wide * 4 + loop
    sibling = loop + 1 - 2 * (loop % 2)
    across = (loop + 2) % 4
    across_sibling = (sibling + 2) % 4
    interior = (wide % 3) != 0
    ends = (wide % 3) == 0
    high = wide // 2
    source = [wide, wide + 1 - 2 * (wide % 2), 2 - high, 3 - 3 * high]
    middle = 3 - wide
    outer = (wide - 1) * 3
    size = rows // PARTS
    parts = range(PARTS)

    load_image = pltpu.make_async_copy(image_hbm, image_raw, load_sem.at[0])
    load_text = pltpu.make_async_copy(text_hbm, text_raw, load_sem.at[1])
    load_pair = pltpu.make_async_copy(pair_hbm, pair_raw, load_sem.at[2])
    load_image.start()
    load_pair.start()
    load_text.start()
    load_scale = pltpu.make_async_copy(scale_hbm, scale_ref, load_sem.at[3])
    load_bias = pltpu.make_async_copy(bias_hbm, bias_ref, load_sem.at[4])
    load_scale.start()
    load_bias.start()

    barrier = pltpu.get_barrier_semaphore()

    def peer(step):
        other = (me + step) % 16
        return {"wide": other // 4, "loop": other % 4}

    for step in range(1, 16):
        pl.semaphore_signal(barrier, inc=1, device_id=peer(step), device_id_type=MESH)

    def block(place, column, part):
        slot = (place * 4 + column) * PARTS + part
        return slot, gathered.at[pl.ds(pl.multiple_of(slot * size, size), size), :]

    load_image.wait()
    image = image_raw[...].astype(jnp.float32)
    image_inverse = lax.rsqrt(jnp.sum(image * image, axis=1, keepdims=True) + epsilon)
    gathered[pl.ds(pl.multiple_of(me * rows, rows), rows), :] = (image * image_inverse).astype(
        jnp.bfloat16
    )
    load_pair.wait()
    pair_all[me] = jnp.concatenate([pair_raw[...], jnp.zeros((1, 128 - rows), jnp.int32)], axis=1)
    pl.semaphore_wait(barrier, 15)

    def send(number, place, column, part, to):
        slot, view = block(place, column, part)
        pltpu.make_async_remote_copy(
            src_ref=view,
            dst_ref=view,
            send_sem=send_sem.at[number * PARTS + part],
            recv_sem=recv_sem.at[slot],
            device_id=to,
            device_id_type=MESH,
        ).start()

    def sent(number):
        view = gathered.at[pl.ds(0, size), :]
        for part in parts:
            pltpu.make_async_copy(view, view, send_sem.at[number * PARTS + part]).wait()

    def arrived(place, column, part):
        slot, view = block(place, column, part)
        pltpu.make_async_copy(view, view, recv_sem.at[slot]).wait()

    for part in parts:
        send(2, wide, loop, part, {"wide": wide, "loop": across})
        send(0, wide, loop, part, {"wide": source[1], "loop": loop})

        @pl.when(interior)
        def _():
            send(1, wide, loop, part, {"wide": middle, "loop": loop})

    for part in parts:
        send(3, wide, loop, part, {"wide": wide, "loop": sibling})
    for step in range(1, 16):
        pltpu.make_async_remote_copy(
            src_ref=pair_all.at[me],
            dst_ref=pair_all.at[me],
            send_sem=small_send.at[0],
            recv_sem=small_recv.at[0],
            device_id=peer(step),
            device_id_type=MESH,
        ).start()

    load_text.wait()
    text = text_raw[...].astype(jnp.float32)
    inverse = lax.rsqrt(jnp.sum(text * text, axis=1, keepdims=True) + epsilon)
    text_bf[...] = (text * inverse).astype(jnp.bfloat16)
    load_scale.wait()
    load_bias.wait()
    scale_value = scale_ref[0]
    bias_value = bias_ref[0]

    def pass_on(k, part):
        arrived(source[k], loop, part)

        @pl.when(interior)
        def _():
            send(
                4 + k,
                source[k],
                loop,
                part,
                {"wide": middle if k == 1 else outer, "loop": loop},
            )

        send(8 + k, source[k], loop, part, {"wide": wide, "loop": across})
        send(12 + k, source[k], loop, part, {"wide": wide, "loop": sibling})

    def pass_across(k, part):
        arrived(source[k], across, part)
        send(16 + k, source[k], across, part, {"wide": wide, "loop": sibling})

    def siblings(k):
        for part in parts:
            arrived(source[k], sibling, part)
        for part in parts:
            arrived(source[k], across_sibling, part)

    columns = me * rows + lax.broadcasted_iota(jnp.int32, (rows, 4 * rows), 0)

    def terms(k):
        place = source[k]
        images = gathered[pl.ds(pl.multiple_of(place * 4 * rows, 4 * rows), 4 * rows), :]
        scores = lax.dot_general(
            text_bf[...], images, (((1,), (1,)), ((), ())), preferred_element_type=jnp.float32
        )
        logits = scale_value * scores + bias_value
        positive = pair_rows[pl.ds(place, 1), :] == columns
        small = jnp.exp(-jnp.abs(logits))
        above = 1.0 + small
        lost = above == 1.0
        log_above = jnp.where(
            lost, small, jnp.log(above) * small / jnp.where(lost, 1.0, above - 1.0)
        )
        loss = log_above + jnp.maximum(jnp.where(positive, -logits, logits), 0.0)
        sigmoid = jnp.where(logits >= 0.0, 1.0, small) / above
        weights = (scale_value * (sigmoid - jnp.where(positive, 1.0, 0.0))).astype(jnp.bfloat16)
        tile = loss[:, :128] + loss[:, 128:]
        tile = jnp.sum(tile.reshape(rows // 8, 8, 128), axis=0)
        return tile, weights, images

    def accumulate(k, weights, images):
        partial = jnp.dot(weights, images, preferred_element_type=jnp.float32)
        if k == 0:
            total[...] = partial
        else:
            total[...] += partial

    for part in parts:
        pass_on(1, part)

        @pl.when(interior)
        def _():
            pass_on(2, part)

        pass_across(0, part)
    fifteen = pair_all.at[pl.ds(0, 15)]
    pltpu.make_async_copy(fifteen, fifteen, small_recv.at[0]).wait()
    for place in range(4):
        pair_rows[place : place + 1, :] = jnp.concatenate(
            [pair_all[place * 4 + column][:, :rows] for column in range(4)], axis=1
        )
    siblings(0)
    tile, weights, images = terms(0)
    accumulate(0, weights, images)
    loss_tile = tile

    for part in parts:

        @pl.when(ends)
        def _():
            pass_on(2, part)

        @pl.when(interior)
        def _():
            pass_on(3, part)

        pass_across(1, part)
    siblings(1)
    tile, weights, images = terms(1)
    accumulate(1, weights, images)
    loss_tile += tile

    for part in parts:

        @pl.when(ends)
        def _():
            pass_on(3, part)

        pass_across(2, part)
    siblings(2)
    tile, weights, images = terms(2)
    accumulate(2, weights, images)
    loss_tile += tile

    for part in parts:
        pass_across(3, part)
    siblings(3)
    tile, weights, images = terms(3)
    loss_tile += tile
    loss_mine[...] = jnp.sum(loss_tile, axis=0, keepdims=True)
    for step in range(1, 16):
        pltpu.make_async_remote_copy(
            src_ref=loss_mine,
            dst_ref=loss_all.at[step - 1],
            send_sem=small_send.at[1],
            recv_sem=small_recv.at[1],
            device_id=peer(step),
            device_id_type=MESH,
        ).start()
    unit_grad = total[...] + jnp.dot(weights, images, preferred_element_type=jnp.float32)
    text = text_raw[...].astype(jnp.float32)
    inverse = lax.rsqrt(jnp.sum(text * text, axis=1, keepdims=True) + epsilon)
    text_hat = text * inverse
    along = jnp.sum(text_hat * unit_grad, axis=1, keepdims=True)
    grad_ref[...] = (unit_grad - text_hat * along) * inverse

    for number in (0, 2, 3, 9, 10, 11, 13, 14, 15, 16, 17, 18, 19):
        sent(number)

    @pl.when(interior)
    def _():
        for number in (1, 5, 6, 7):
            sent(number)

    pltpu.make_async_copy(fifteen, fifteen, small_send.at[0]).wait()
    pltpu.make_async_copy(loss_all, loss_all, small_send.at[1]).wait()
    pltpu.make_async_copy(loss_all, loss_all, small_recv.at[1]).wait()
    whole = loss_mine[...] + jnp.sum(loss_all[...], axis=0)
    loss_ref[0] = jnp.sum(whole) * (1.0 / float((16 * rows) ** 2))


def gather_shards(image_embed, text_embed, pair_index, logit_scale, logit_bias):
    rows, width = text_embed.shape
    vmem = pl.BlockSpec(memory_space=pltpu.VMEM)
    smem = pl.BlockSpec(memory_space=pltpu.SMEM)
    hbm = pl.BlockSpec(memory_space=pltpu.HBM)
    return pl.pallas_call(
        functools.partial(gather_kernel, rows),
        out_shape=(
            pltpu.VMEM((rows, width), jnp.float32),
            jax.ShapeDtypeStruct((1,), jnp.float32),
        ),
        in_specs=[hbm, hbm, hbm, hbm, hbm],
        out_specs=(vmem, smem),
        scratch_shapes=[
            pltpu.VMEM((16 * rows, width), jnp.bfloat16),
            pltpu.VMEM((rows, width), jnp.bfloat16),
            pltpu.VMEM((rows, width), jnp.bfloat16),
            pltpu.VMEM((1, rows), jnp.int32),
            pltpu.VMEM((16, 1, 128), jnp.int32),
            pltpu.VMEM((8, 4 * rows), jnp.int32),
            pltpu.VMEM((15, 1, 128), jnp.float32),
            pltpu.VMEM((1, 128), jnp.float32),
            pltpu.VMEM((rows, width), jnp.bfloat16),
            pltpu.VMEM((rows, width), jnp.float32),
            pltpu.SMEM((1,), jnp.float32),
            pltpu.SMEM((1,), jnp.float32),
            pltpu.SemaphoreType.DMA((5,)),
            pltpu.SemaphoreType.DMA((20 * PARTS,)),
            pltpu.SemaphoreType.DMA((16 * PARTS,)),
            pltpu.SemaphoreType.DMA((2,)),
            pltpu.SemaphoreType.DMA((2,)),
        ],
        compiler_params=pltpu.CompilerParams(
            collective_id=0, has_side_effects=True, vmem_limit_bytes=60 * 1024 * 1024
        ),
    )(image_embed, text_embed, pair_index.reshape(1, rows), logit_scale, logit_bias)


def solution(mesh):
    small = mesh.shape["wide"] == 4 and mesh.shape["loop"] == 4
    return jax.shard_map(
        gather_shards if small else ring_shards,
        mesh=mesh,
        in_specs=(
            P(("groups", "wide", "loop"), None),
            P(("groups", "wide", "loop"), None),
            P(("groups", "wide", "loop")),
            P(),
            P(),
        ),
        out_specs=(P(("groups", "wide", "loop"), None), P("groups")),
        check_vma=False,
    )
```

```python
import functools

import jax
import jax.numpy as jnp
from jax import lax
from jax.experimental import pallas as pl
from jax.experimental.pallas import tpu as pltpu
from jax.sharding import PartitionSpec as P

epsilon = 1e-06
MESH = pl.DeviceIdType.MESH


def passed_along(block, axis, distance):
    devices = range(lax.axis_size(axis))
    route = [((i - distance) % len(devices), i) for i in devices]
    return lax.ppermute(block, axis, route)


def normalize(values):
    wide_values = values.astype(jnp.float32)
    inverse = lax.rsqrt(jnp.sum(wide_values * wide_values, axis=1, keepdims=True) + epsilon)
    return (wide_values * inverse, inverse)


def pair_terms(text_block, first_row, image_bf, pairs, scale_value, bias_value):
    scores = lax.dot_general(
        text_block, image_bf, (((1,), (1,)), ((), ())), preferred_element_type=jnp.float32
    )
    logits = scale_value * scores + bias_value
    columns = first_row + lax.broadcasted_iota(jnp.int32, (text_block.shape[0], 1), 0)
    positive = pairs[None, :] == columns
    signed = jnp.where(positive, logits, -logits)
    loss_part = -jnp.sum(jax.nn.log_sigmoid(signed))
    weights = (scale_value * (jax.nn.sigmoid(logits) - positive.astype(jnp.float32))).astype(
        jnp.bfloat16
    )
    partial_sum = jnp.dot(weights, image_bf, preferred_element_type=jnp.float32)
    return (loss_part, partial_sum)


def ring_shards(image_embed, text_embed, pair_index, logit_scale, logit_bias):
    local_rows = text_embed.shape[0]
    width_dim = text_embed.shape[1]
    loop_size = lax.axis_size("loop")
    loop_index = lax.axis_index("loop")
    wide_index = lax.axis_index("wide")
    scale_value = logit_scale[0]
    bias_value = logit_bias[0]
    image_unit, _ = normalize(image_embed)
    image_bf = image_unit.astype(jnp.bfloat16)
    text_hat, inverse = normalize(text_embed)
    text_bf = text_hat.astype(jnp.bfloat16)
    group_first = wide_index * loop_size * local_rows
    gathered, gathered_pairs = (
        lax.all_gather(image_bf, "wide", axis=0, tiled=True),
        lax.all_gather(pair_index, "wide", axis=0, tiled=True),
    )
    loss_sum = jnp.zeros((), jnp.float32)
    text_block = text_bf
    accumulated = jnp.zeros((local_rows, width_dim), jnp.float32)
    for cycle_step in range(loop_size):
        owner_block = (loop_index - cycle_step) % loop_size
        first_row = group_first + owner_block * local_rows
        loss_part, partial_sum = pair_terms(
            text_block, first_row, gathered, gathered_pairs, scale_value, bias_value
        )
        loss_sum = loss_sum + loss_part
        accumulated = accumulated + partial_sum
        if cycle_step + 1 < loop_size:
            text_block = passed_along(text_block, "loop", 1)
            accumulated = passed_along(accumulated, "loop", 1)
    unit_grad = passed_along(accumulated, "loop", 1)
    along = jnp.sum(text_hat * unit_grad, axis=1, keepdims=True)
    text_grad = (unit_grad - text_hat * along) * inverse
    pairs_total = float(local_rows * lax.axis_size("wide") * loop_size)
    total_loss = lax.psum(loss_sum, ("wide", "loop"))
    mean_loss = jnp.reshape(total_loss / (pairs_total * pairs_total), (1,))
    return (text_grad, mean_loss)


PARTS = 2


def gather_kernel(
    rows,
    image_hbm,
    text_hbm,
    pair_hbm,
    scale_hbm,
    bias_hbm,
    grad_ref,
    loss_ref,
    gathered,
    image_raw,
    text_raw,
    pair_raw,
    pair_all,
    pair_rows,
    loss_all,
    loss_mine,
    text_bf,
    total,
    scale_ref,
    bias_ref,
    load_sem,
    send_sem,
    recv_sem,
    small_send,
    small_recv,
):
    wide, loop = lax.axis_index("wide"), lax.axis_index("loop")
    me = wide * 4 + loop
    sibling = loop + 1 - 2 * (loop % 2)
    across = (loop + 2) % 4
    across_sibling = (sibling + 2) % 4
    interior = (wide % 3) != 0
    ends = (wide % 3) == 0
    high = wide // 2
    source = [wide, wide + 1 - 2 * (wide % 2), 2 - high, 3 - 3 * high]
    middle = 3 - wide
    outer = (wide - 1) * 3
    size = rows // PARTS
    parts = range(PARTS)

    load_image = pltpu.make_async_copy(image_hbm, image_raw, load_sem.at[0])
    load_text = pltpu.make_async_copy(text_hbm, text_raw, load_sem.at[1])
    load_pair = pltpu.make_async_copy(pair_hbm, pair_raw, load_sem.at[2])
    load_image.start()
    load_pair.start()
    load_text.start()
    load_scale = pltpu.make_async_copy(scale_hbm, scale_ref, load_sem.at[3])
    load_bias = pltpu.make_async_copy(bias_hbm, bias_ref, load_sem.at[4])
    load_scale.start()
    load_bias.start()

    barrier = pltpu.get_barrier_semaphore()

    def peer(step):
        other = (me + step) % 16
        return {"wide": other // 4, "loop": other % 4}

    for step in range(1, 16):
        pl.semaphore_signal(barrier, inc=1, device_id=peer(step), device_id_type=MESH)

    def block(place, column, part):
        slot = (place * 4 + column) * PARTS + part
        return slot, gathered.at[pl.ds(pl.multiple_of(slot * size, size), size), :]

    load_image.wait()
    image = image_raw[...].astype(jnp.float32)
    image_inverse = lax.rsqrt(jnp.sum(image * image, axis=1, keepdims=True) + epsilon)
    gathered[pl.ds(pl.multiple_of(me * rows, rows), rows), :] = (image * image_inverse).astype(
        jnp.bfloat16
    )
    load_pair.wait()
    pair_all[me] = jnp.concatenate([pair_raw[...], jnp.zeros((1, 128 - rows), jnp.int32)], axis=1)
    pl.semaphore_wait(barrier, 15)

    def send(number, place, column, part, to):
        slot, view = block(place, column, part)
        pltpu.make_async_remote_copy(
            src_ref=view,
            dst_ref=view,
            send_sem=send_sem.at[number * PARTS + part],
            recv_sem=recv_sem.at[slot],
            device_id=to,
            device_id_type=MESH,
        ).start()

    def sent(number):
        view = gathered.at[pl.ds(0, size), :]
        for part in parts:
            pltpu.make_async_copy(view, view, send_sem.at[number * PARTS + part]).wait()

    def arrived(place, column, part):
        slot, view = block(place, column, part)
        pltpu.make_async_copy(view, view, recv_sem.at[slot]).wait()

    for part in parts:
        send(2, wide, loop, part, {"wide": wide, "loop": across})
        send(0, wide, loop, part, {"wide": source[1], "loop": loop})

        @pl.when(interior)
        def _():
            send(1, wide, loop, part, {"wide": middle, "loop": loop})

    for part in parts:
        send(3, wide, loop, part, {"wide": wide, "loop": sibling})
    for step in range(1, 16):
        pltpu.make_async_remote_copy(
            src_ref=pair_all.at[me],
            dst_ref=pair_all.at[me],
            send_sem=small_send.at[0],
            recv_sem=small_recv.at[0],
            device_id=peer(step),
            device_id_type=MESH,
        ).start()

    load_text.wait()
    text = text_raw[...].astype(jnp.float32)
    inverse = lax.rsqrt(jnp.sum(text * text, axis=1, keepdims=True) + epsilon)
    text_bf[...] = (text * inverse).astype(jnp.bfloat16)
    load_scale.wait()
    load_bias.wait()
    scale_value = scale_ref[0]
    bias_value = bias_ref[0]

    def pass_on(k, part):
        arrived(source[k], loop, part)

        @pl.when(interior)
        def _():
            send(
                4 + k,
                source[k],
                loop,
                part,
                {"wide": middle if k == 1 else outer, "loop": loop},
            )

        send(8 + k, source[k], loop, part, {"wide": wide, "loop": across})
        send(12 + k, source[k], loop, part, {"wide": wide, "loop": sibling})

    def pass_across(k, part):
        arrived(source[k], across, part)
        send(16 + k, source[k], across, part, {"wide": wide, "loop": sibling})

    def siblings(k, column):
        for part in parts:
            arrived(source[k], column, part)

    lanes = 2 * rows

    def terms(k, column=None):
        place = source[k]
        if column is None:
            first, count = place * 2, 2
        else:
            first, count = place * 2 + column // 2, 1
        images = gathered[pl.ds(pl.multiple_of(first * lanes, lanes), count * lanes), :]
        scores = lax.dot_general(
            text_bf[...], images, (((1,), (1,)), ((), ())), preferred_element_type=jnp.float32
        )
        logits = scale_value * scores + bias_value
        columns = me * rows + lax.broadcasted_iota(jnp.int32, logits.shape, 0)
        held = [pair_rows[pl.ds(first + i, 1), :] for i in range(count)]
        positive = (held[0] if count == 1 else jnp.concatenate(held, axis=1)) == columns
        small = jnp.exp(-jnp.abs(logits))
        above = 1.0 + small
        lost = above == 1.0
        log_above = jnp.where(
            lost, small, jnp.log(above) * small / jnp.where(lost, 1.0, above - 1.0)
        )
        loss = log_above + jnp.maximum(jnp.where(positive, -logits, logits), 0.0)
        sigmoid = jnp.where(logits >= 0.0, 1.0, small) / above
        weights = (scale_value * (sigmoid - jnp.where(positive, 1.0, 0.0))).astype(jnp.bfloat16)
        tile = loss if count == 1 else loss[:, :lanes] + loss[:, lanes:]
        tile = jnp.sum(tile.reshape(rows // 8, 8, lanes), axis=0)
        return tile, weights, images

    def accumulate(weights, images):
        total[...] += jnp.dot(weights, images, preferred_element_type=jnp.float32)

    for part in parts:
        pass_on(1, part)

        @pl.when(interior)
        def _():
            pass_on(2, part)

        pass_across(0, part)
    fifteen = pair_all.at[pl.ds(0, 15)]
    pltpu.make_async_copy(fifteen, fifteen, small_recv.at[0]).wait()
    for chip in range(8):
        pair_rows[chip : chip + 1, :] = jnp.concatenate(
            [pair_all[chip * 2 + core][:, :rows] for core in range(2)], axis=1
        )
    siblings(0, sibling)
    siblings(0, across_sibling)
    loss_tile, weights, images = terms(0)
    total[...] = jnp.dot(weights, images, preferred_element_type=jnp.float32)

    for part in parts:

        @pl.when(ends)
        def _():
            pass_on(2, part)

        @pl.when(interior)
        def _():
            pass_on(3, part)

        pass_across(1, part)
    siblings(1, sibling)
    tile, weights, images = terms(1, loop)
    accumulate(weights, images)
    loss_tile += tile

    for part in parts:

        @pl.when(ends)
        def _():
            pass_on(3, part)

        pass_across(2, part)
    siblings(2, sibling)
    siblings(2, across_sibling)
    tile, weights, images = terms(2)
    accumulate(weights, images)
    loss_tile += tile
    siblings(3, sibling)
    tile, weights, images = terms(3, loop)
    accumulate(weights, images)
    loss_tile += tile

    for part in parts:
        pass_across(3, part)
    siblings(1, across_sibling)
    tile, weights, images = terms(1, across)
    accumulate(weights, images)
    loss_tile += tile
    siblings(3, across_sibling)
    tile, weights, images = terms(3, across)
    loss_tile += tile
    loss_mine[...] = jnp.sum(loss_tile, axis=0, keepdims=True)
    for step in range(1, 16):
        pltpu.make_async_remote_copy(
            src_ref=loss_mine,
            dst_ref=loss_all.at[step - 1],
            send_sem=small_send.at[1],
            recv_sem=small_recv.at[1],
            device_id=peer(step),
            device_id_type=MESH,
        ).start()
    unit_grad = total[...] + jnp.dot(weights, images, preferred_element_type=jnp.float32)
    text = text_raw[...].astype(jnp.float32)
    inverse = lax.rsqrt(jnp.sum(text * text, axis=1, keepdims=True) + epsilon)
    text_hat = text * inverse
    along = jnp.sum(text_hat * unit_grad, axis=1, keepdims=True)
    grad_ref[...] = (unit_grad - text_hat * along) * inverse

    for number in (0, 2, 3, 9, 10, 11, 13, 14, 15, 16, 17, 18, 19):
        sent(number)

    @pl.when(interior)
    def _():
        for number in (1, 5, 6, 7):
            sent(number)

    pltpu.make_async_copy(fifteen, fifteen, small_send.at[0]).wait()
    pltpu.make_async_copy(loss_all, loss_all, small_send.at[1]).wait()
    pltpu.make_async_copy(loss_all, loss_all, small_recv.at[1]).wait()
    whole = loss_mine[...] + jnp.sum(loss_all[...], axis=0)
    loss_ref[0] = jnp.sum(whole) * (1.0 / float((16 * rows) ** 2))


def gather_shards(image_embed, text_embed, pair_index, logit_scale, logit_bias):
    rows, width = text_embed.shape
    vmem = pl.BlockSpec(memory_space=pltpu.VMEM)
    smem = pl.BlockSpec(memory_space=pltpu.SMEM)
    hbm = pl.BlockSpec(memory_space=pltpu.HBM)
    return pl.pallas_call(
        functools.partial(gather_kernel, rows),
        out_shape=(
            pltpu.VMEM((rows, width), jnp.float32),
            jax.ShapeDtypeStruct((1,), jnp.float32),
        ),
        in_specs=[hbm, hbm, hbm, hbm, hbm],
        out_specs=(vmem, smem),
        scratch_shapes=[
            pltpu.VMEM((16 * rows, width), jnp.bfloat16),
            pltpu.VMEM((rows, width), jnp.bfloat16),
            pltpu.VMEM((rows, width), jnp.bfloat16),
            pltpu.VMEM((1, rows), jnp.int32),
            pltpu.VMEM((16, 1, 128), jnp.int32),
            pltpu.VMEM((8, 2 * rows), jnp.int32),
            pltpu.VMEM((15, 1, 128), jnp.float32),
            pltpu.VMEM((1, 128), jnp.float32),
            pltpu.VMEM((rows, width), jnp.bfloat16),
            pltpu.VMEM((rows, width), jnp.float32),
            pltpu.SMEM((1,), jnp.float32),
            pltpu.SMEM((1,), jnp.float32),
            pltpu.SemaphoreType.DMA((5,)),
            pltpu.SemaphoreType.DMA((20 * PARTS,)),
            pltpu.SemaphoreType.DMA((16 * PARTS,)),
            pltpu.SemaphoreType.DMA((2,)),
            pltpu.SemaphoreType.DMA((2,)),
        ],
        compiler_params=pltpu.CompilerParams(
            collective_id=0, has_side_effects=True, vmem_limit_bytes=60 * 1024 * 1024
        ),
    )(image_embed, text_embed, pair_index.reshape(1, rows), logit_scale, logit_bias)


def solution(mesh):
    small = mesh.shape["wide"] == 4 and mesh.shape["loop"] == 4
    return jax.shard_map(
        gather_shards if small else ring_shards,
        mesh=mesh,
        in_specs=(
            P(("groups", "wide", "loop"), None),
            P(("groups", "wide", "loop"), None),
            P(("groups", "wide", "loop")),
            P(),
            P(),
        ),
        out_specs=(P(("groups", "wide", "loop"), None), P("groups")),
        check_vma=False,
    )
```
